128 devices in a mesh: blk: 4 (over y_hi, core), ga: 32 (over x, y_lo, z).
Axes of the slice: x: 4, y: 4 (y_hi: 2, y_lo: 2; y = y_hi * 2 + y_lo), z: 4, core: 2. Of those that a mesh axis runs over, the one named last changes fastest.
Arguments:
- screening: bfloat16 [16384, 16384], P('ga', 'blk'), as said below
- pair_elements: bfloat16 [16384, 2048], P('ga', 'blk'), may hold values from -6 to 6
- summed_bands: int32 [16], P('blk'), may hold values from 0 to 2047
- occupied: int32 [1], replicated, may hold values from 768 to 1280
Outputs:
- sigma: float32 [128, 128], P(('blk', 'ga'))
The draws below stay inside these ranges and needn't reach their ends.
Inputs may be any that keep to these rules, and one draw needn't show every extreme that they name: screening is symmetric: screening[G, G'] = screening[G', G]; its diagonal lies between 0.3 and 3 and its off-diagonal entries have magnitude at most 4 / sqrt(16384).
All inputs are finite; a program needn't handle non-finite values.
Results may differ from the reference program's by a relative error of at most 0.0017.
Values may be sent and summed in bfloat16 or wider, within the bound.
No kernel may reach another device: no remote copies, remote signals or barrier semaphores. Data moves between devices by JAX's collectives and lax.ppermute only.
A program may use at most 128 MiB of HBM per device.

```python
import math
import jax
import jax.numpy as jnp

NG = 16384
NS = 128
NM = 16


def draw_screening(key, part):
    key = jax.random.fold_in(key, 11)
    key_off, key_diag = jax.random.split(key)
    raw = jnp.clip(jax.random.normal(key_off, (NG, NG), jnp.float32), -4.0, 4.0)
    off_part = (raw + raw.T) * (0.5 / jnp.sqrt(jnp.float32(NG)))
    diag_vals = jnp.exp(jax.random.uniform(key_diag, (NG,), jnp.float32, jnp.log(0.3), jnp.log(3.0)))
    rows = grid_index(NG)
    same = rows[:, None] == rows[None, :]
    return jnp.where(same, diag_vals[:, None], off_part).astype(jnp.bfloat16)


def grid_index(count):
    return jnp.arange(count, dtype=jnp.int32)


def set_ends(result, rng, least, high):
    spot = [jax.random.randint(jax.random.fold_in(rng, axis), (), 0, length) for axis, length in enumerate(result.shape)]
    longest = result.shape.index(max(result.shape))
    neighbour = spot[:longest] + [(spot[longest] + 1) % result.shape[longest]] + spot[longest + 1:]
    return result.at[tuple(spot)].set(least).at[tuple(neighbour)].set(high)


def levels(stream_key, dims, shards, low, high):
    loudness = 1.0
    for axis_at, parts in shards:
        draws = jax.random.uniform(jax.random.fold_in(jax.random.fold_in(stream_key, 6), axis_at), (parts,), jnp.float32, low / len(shards), high / len(shards))
        loudness = loudness * jnp.repeat(jnp.exp(draws), dims[axis_at] // parts).reshape((-1,) + (1,) * (len(dims) - 1 - axis_at))
    return loudness


def scatter_about(rng, extent, width, limit, pieces=(), held_as=jnp.bfloat16):
    result = jax.random.normal(rng, extent, jnp.float32) * width
    if len(pieces) > 0:
        result = levels(rng, extent, pieces, -0.22, 0.18) * result
    return jnp.clip(result, min=-limit, max=limit).astype(held_as)


def setup_inputs(seed: int = 0) -> dict:
    keys = jax.random.split(jax.random.key(seed), 5)
    screening = draw_screening(jax.random.fold_in(keys[4], 71), 0)
    pair_elements = scatter_about(keys[1], (NG, NM * NS), 1.0, 6.0, ((0, 32), (1, 4)))
    summed_bands = set_ends(jax.random.randint(keys[2], (NM,), 0, 2048), jax.random.fold_in(keys[2], 1), 0, 2047).astype(jnp.int32)
    occupied = jax.random.randint(keys[3], (1,), 768, 1281).astype(jnp.int32)
    return {"screening": screening, "pair_elements": pair_elements, "summed_bands": summed_bands, "occupied": occupied}


def reference(screening, pair_elements, summed_bands, occupied):
    screened = jnp.dot(screening, pair_elements, preferred_element_type=jnp.float32)
    weight = jnp.where(summed_bands < occupied[0], -0.5, 0.5).astype(jnp.float32)
    count_bands = summed_bands.shape[0]
    weighted = (screened.reshape(NG, count_bands, NS) * weight[None, :, None]).astype(jnp.bfloat16)
    elements = pair_elements.reshape(NG, count_bands, NS).astype(jnp.float32)
    total = jnp.einsum('gmn,gmk->nk', elements, weighted.astype(jnp.float32))
    return total / jnp.float32(math.sqrt(NG * count_bands))
```

```python
import math

import jax
import jax.numpy as jnp
from jax import lax
from jax.sharding import PartitionSpec as P

NS = 128
AXES = ("blk", "ga")


def place(x, y, z, core):
    return ((y // 2) * 2 + core) * 32 + (x % 4) * 8 + (y % 2) * 4 + z % 4


def pairs(target, keep=lambda x, y, z, core: True):
    return [
        (place(x, y, z, core), place(*target(x, y, z, core)))
        for x in range(4)
        for y in range(4)
        for z in range(4)
        for core in range(2)
        if keep(x, y, z, core)
    ]


def inner(x, y):
    return x // 2 == y // 2


def far_core(x, y):
    return 1 - (x if inner(x, y) else 3 - x) % 2


def is_inner(x, y, z, core):
    return inner(x, y)


def is_far(x, y, z, core):
    return core == far_core(x, y)


def to_near_plane(x, y, z, core):
    return (3 - x, y, z, core) if inner(x, y) else (x, (y + 2) % 4, z, core)


def to_partner(x, y, z, core):
    return x ^ 1, y, z, far_core(x ^ 1, y)


CORE = pairs(lambda x, y, z, core: (x, y, z, 1 - core))
INJECT = pairs(to_near_plane)
PARTNER = pairs(to_partner, is_far)
PARTNER_INNER = pairs(to_partner, lambda x, y, z, core: is_far(x, y, z, core) and inner(x, y))
SIDE = pairs(lambda x, y, z, core: (x, y ^ 1, z, core))
SIDE_INNER = pairs(lambda x, y, z, core: (x, y ^ 1, z, core), is_inner)
DOWN = pairs(lambda x, y, z, core: (x, y, z - 1, core))
UP = pairs(lambda x, y, z, core: (x, y, z + 1, core))


def send(value, table):
    return lax.ppermute(value, AXES, table)


def shards(screening, pair_elements, summed_bands, occupied):
    rows = pair_elements.shape[0]
    bands = summed_bands.shape[0]
    total_g = rows * lax.axis_size("ga")
    scale = 1.0 / math.sqrt(total_g * bands * lax.axis_size("blk"))
    blk, ga = lax.axis_index("blk"), lax.axis_index("ga")
    y_hi, core = blk // 2, blk % 2
    x, y_lo, z = ga // 8, (ga // 4) % 2, ga % 4
    at_inner = x // 2 == y_hi
    near_plane = jnp.where(at_inner, x, 3 - x)
    near = core == near_plane % 2

    weight = jnp.where(summed_bands < occupied[0], -0.5, 0.5).astype(jnp.bfloat16)
    wide = jnp.broadcast_to(jnp.repeat(weight, NS)[None, :], (16, bands * NS))

    swapped = send(screening, PARTNER)
    own = pair_elements
    brought = send(own, INJECT)
    brought_wide = send(wide, INJECT)
    own_weighted = own * wide[:1]
    own_weighted_other = send(own_weighted, CORE)
    native = jnp.where(at_inner, own, brought)
    own_side = send(own, SIDE_INNER)
    up_1 = send(native, DOWN)
    down_1 = send(brought, UP)
    brought_side = send(brought, SIDE)
    native_side = jnp.where(at_inner, own_side, brought_side)
    up_2 = send(native_side, DOWN)
    down_2 = send(brought_side, UP)
    side = jnp.where(at_inner & (y_lo == 0), own_side, brought_side)
    across_up = send(jnp.where((z + 3) % 4 < 2, up_1, up_2), DOWN)
    across_down = send(jnp.where((z + 1) % 4 < 2, down_2, down_1), UP)

    brought_weighted = brought * brought_wide[:1]
    brought_weighted_other = send(brought_weighted, CORE)
    native_rows = jnp.concatenate([own_weighted, own_weighted_other], 1)
    foreign_rows = jnp.concatenate([brought_weighted, brought_weighted_other], 1)
    partner_native = jnp.roll(send(native_rows, PARTNER), bands * NS, axis=1)
    partner_foreign = jnp.roll(send(foreign_rows, PARTNER_INNER), bands * NS, axis=1)
    left_a = jnp.where(near, native_rows, partner_native)
    left_b = jnp.where(at_inner, jnp.where(near, foreign_rows, partner_foreign), left_a)

    plain = jnp.where(at_inner, jnp.where(near, 0.5, x % 2), 1.0).astype(jnp.bfloat16)
    odd = jnp.where(at_inner, jnp.where(near, 0.5, 1 - x % 2), 0.0).astype(jnp.bfloat16)
    low = z < 2
    other = 1 - y_lo
    z_up, z_down, z_across = (z + 1) % 4, (z + 3) % 4, (z + 2) % 4
    group_a = [
        (native, y_lo, z, plain),
        (up_1, y_lo, z_up, None),
        (up_2, other, z_up, None),
        (across_up, jnp.where(low, y_lo, other), z_across, None),
    ]
    group_b = [
        (brought, y_lo, z, odd),
        (down_1, y_lo, z_down, None),
        (down_2, other, z_down, None),
        (across_down, jnp.where(low, other, y_lo), z_across, None),
    ]
    group_c = [(side, other, z, None)]
    interaction = jnp.where(near, screening, swapped)

    def screened(group):
        blocks = jnp.concatenate([block for block, _, _, _ in group], 0)
        blocks = jnp.concatenate([blocks, send(blocks, CORE)], 1)
        columns = []
        for _, y_at, z_at, factor in group:
            part = lax.dynamic_slice_in_dim(interaction, (y_at * 4 + z_at) * rows, rows, 1)
            columns.append(part if factor is None else part * factor)
        columns = jnp.concatenate(columns, 1)
        return jnp.dot(columns, blocks, preferred_element_type=jnp.float32)

    def contract(left, right):
        high = lax.reduce_precision(right, 8, 7)
        left = left.reshape(rows, 2 * bands, NS)
        return sum(
            jnp.einsum(
                "gmn,gmk->nk",
                left,
                part.astype(jnp.bfloat16).reshape(rows, 2 * bands, NS),
                preferred_element_type=jnp.float32,
            )
            for part in (high, right - high)
        )

    screened_a, screened_b, screened_c = screened(group_a), screened(group_b), screened(group_c)
    first = (y_lo == 0).astype(jnp.float32)
    half = contract(left_a, screened_a + first * screened_c)
    half = half + contract(left_b, screened_b + (1.0 - first) * screened_c)
    value = (half + half.T) * jnp.float32(scale)
    parts = lax.all_to_all(value.reshape(NS, 1, NS), AXES, 0, 0)
    return jnp.sum(parts, 0)


def solution(mesh):
    placed = (P("ga", "blk"), P("ga", "blk"), P("blk"), P())
    return jax.shard_map(
        shards, mesh=mesh, in_specs=placed, out_specs=P(("blk", "ga"), None), check_vma=False
    )
```

```python
import math

import jax
import jax.numpy as jnp
from jax import lax
from jax.experimental import pallas as pl
from jax.experimental.pallas import tpu as pltpu
from jax.sharding import PartitionSpec as P

NS = 128
AXES = ("blk", "ga")


def place(x, y, z, core):
    return ((y // 2) * 2 + core) * 32 + (x % 4) * 8 + (y % 2) * 4 + z % 4


def pairs(target, keep=lambda x, y, z, core: True):
    return [
        (place(x, y, z, core), place(*target(x, y, z, core)))
        for x in range(4)
        for y in range(4)
        for z in range(4)
        for core in range(2)
        if keep(x, y, z, core)
    ]


def inner(x, y):
    return x // 2 == y // 2


def far_core(x, y):
    return 1 - (x if inner(x, y) else 3 - x) % 2


def is_inner(x, y, z, core):
    return inner(x, y)


def is_far(x, y, z, core):
    return core == far_core(x, y)


def to_near_plane(x, y, z, core):
    return (3 - x, y, z, core) if inner(x, y) else (x, (y + 2) % 4, z, core)


def to_partner(x, y, z, core):
    return x ^ 1, y, z, far_core(x ^ 1, y)


CORE_NEAR = pairs(
    lambda x, y, z, core: (x, y, z, 1 - core), lambda x, y, z, core: not is_far(x, y, z, core)
)
CORE_FAR = pairs(lambda x, y, z, core: (x, y, z, 1 - core), is_far)
INJECT = pairs(to_near_plane)
RETURN = pairs(to_near_plane, lambda x, y, z, core: not inner(x, y))
SWAP = pairs(to_partner, is_far)
PARTNER = pairs(lambda x, y, z, core: (x ^ 1, y, z, core))
SIDE = pairs(lambda x, y, z, core: (x, y ^ 1, z, core))
SIDE_INNER = pairs(lambda x, y, z, core: (x, y ^ 1, z, core), is_inner)


def down(x, y, z, core):
    return x, y, z - 1, core


def up(x, y, z, core):
    return x, y, z + 1, core


DOWN, UP = pairs(down), pairs(up)

SLOTS = 9
NEAR, INNER, SIDE_OWN = range(SLOTS, SLOTS + 3)


def send(value, table):
    return lax.ppermute(value, AXES, table)


def blend(flag, yes, no):
    flag = flag.astype(yes.dtype)
    return yes * flag + no * (1 - flag)


def products(table, factors, near, far, weight_b, blocks, before=None, scale=None):
    (near_w, *near_rows), (far_w, *far_rows) = near, far
    parts = [len(near_w), len(far_w)]
    rows, (depth, width) = sum(part.shape[0] for part in near_w), blocks[0].shape
    bands = width // NS

    def kernel(table, factors, *refs):
        near_refs, refs = refs[: parts[0]], refs[parts[0] :]
        far_refs, refs = refs[: parts[1]], refs[parts[1] :]
        near_a, near_b, far_a, far_b, weight_ref = refs[:5]
        own, brought, own_side, brought_side, up_1, down_1, up_2, down_2 = refs[5:13]
        across_up, across_down = refs[13:15]
        refs = refs[15:]
        if before is not None:
            before_ref, refs = refs[0], refs[1:]
        out, w, q, left, sems = refs

        def choose(flag, yes, no):
            if yes is no:
                copy(*yes)
                return

            @pl.when(table[flag] == 1)
            def _():
                copy(*yes)

            @pl.when(table[flag] == 0)
            def _():
                copy(*no)

        def copy(*triples):
            for source, target, sem in triples:
                pltpu.make_async_copy(source, target, sem).start()

        def part(slot):
            return slot // 4, pl.ds((slot % 4) * depth, depth)

        sources = [
            (INNER, own, brought),
            (INNER, up_1, up_1),
            (INNER, up_2, up_2),
            (INNER, across_up, across_up),
            (INNER, brought, brought),
            (INNER, down_1, down_1),
            (INNER, down_2, down_2),
            (INNER, across_down, across_down),
            (SIDE_OWN, own_side, brought_side),
        ]
        for slot in (8, 0, 1, 2, 3, 4, 5, 6, 7):
            flag, yes, no = sources[slot]
            yes, no = yes.at[pl.ds(0, depth)], no.at[pl.ds(0, depth)] if no is not yes else None
            group, place_in = part(slot)
            target, sem = q.at[group, place_in], sems.at[0, group]
            if no is None:
                copy((yes, target, sem))
            else:
                choose(flag, [(yes, target, sem)], [(no, target, sem)])
            columns = pl.ds(pl.multiple_of(table[slot] * depth, depth), depth)
            copies = []
            for side in (near_refs, far_refs):
                at, triples = 0, []
                for ref in side:
                    target = w.at[group, pl.ds(at, ref.shape[0]), place_in]
                    triples.append((ref.at[:, columns], target, sems.at[1, group]))
                    at += ref.shape[0]
                copies.append(triples)
            choose(NEAR, *copies)
        block = pl.ds(0, rows)
        targets = [(left.at[group], sems.at[group, 3]) for group in range(2)]
        choose(
            NEAR,
            [(near_a.at[block], *targets[0]), (near_b.at[block], *targets[1])],
            [(far_a.at[block], *targets[0]), (far_b.at[block], *targets[1])],
        )

        def wait(ref, sem):
            pltpu.make_async_copy(ref, ref, sem).wait()

        wait(q.at[2, pl.ds(0, depth)], sems.at[0, 2])
        wait(w.at[2, :, pl.ds(0, depth)], sems.at[1, 2])
        side = jnp.dot(w[2, :, :depth], q[2, :depth], preferred_element_type=jnp.float32)
        result = jnp.zeros((NS, 2 * NS), jnp.float32)
        for group in range(2):
            wait(q.at[group], sems.at[0, group])
            wait(w.at[group], sems.at[1, group])
            q[group, :depth] = q[group, :depth] * factors[group].astype(q.dtype)
            total = jnp.dot(w[group], q[group], preferred_element_type=jnp.float32)
            total = total + side * factors[2 + group]
            if group == 1:
                total = total * weight_ref[0:1, :].astype(jnp.float32)
            high = total.astype(jnp.bfloat16)
            low = (total - high.astype(jnp.float32)).astype(jnp.bfloat16)
            wait(left.at[group], sems.at[group, 3])
            for band in range(bands):
                lanes = slice(band * NS, (band + 1) * NS)
                result = result + lax.dot_general(
                    left[group, :, lanes],
                    jnp.concatenate([high[:, lanes], low[:, lanes]], 1),
                    (((0,), (0,)), ((), ())),
                    preferred_element_type=jnp.float32,
                )
        result = result[:, :NS] + result[:, NS:]
        if before is not None:
            result = result + before_ref[...]
            result = (result + result.T) * jnp.float32(scale)
        out[...] = result

    hbm = pl.BlockSpec(memory_space=pl.ANY)
    vmem = pl.BlockSpec(memory_space=pltpu.VMEM)
    smem = pl.BlockSpec(memory_space=pltpu.SMEM)
    more = [] if before is None else [before]
    return pl.pallas_call(
        kernel,
        out_shape=jax.ShapeDtypeStruct((NS, NS), jnp.float32),
        in_specs=[smem, smem] + [hbm] * (sum(parts) + 4) + [vmem] + [hbm] * 10 + [vmem] * len(more),
        out_specs=vmem,
        scratch_shapes=[
            pltpu.VMEM((3, rows, 4 * depth), jnp.bfloat16),
            pltpu.VMEM((3, 4 * depth, width), jnp.bfloat16),
            pltpu.VMEM((2, rows, width), jnp.bfloat16),
            pltpu.SemaphoreType.DMA((2, 4)),
        ],
        compiler_params=pltpu.CompilerParams(vmem_limit_bytes=60 * 1024 * 1024),
        cost_estimate=pl.CostEstimate(
            flops=2 * SLOTS * rows * depth * width,
            bytes_accessed=2 * SLOTS * (rows + width) * depth,
            transcendentals=0,
        ),
    )(table, factors, *near_w, *far_w, *near_rows, *far_rows, weight_b, *blocks, *more)


def shards(screening, pair_elements, summed_bands, occupied):
    rows = pair_elements.shape[0]
    bands = summed_bands.shape[0]
    total_g = rows * lax.axis_size("ga")
    scale = 1.0 / math.sqrt(total_g * bands * lax.axis_size("blk"))
    blk, ga = lax.axis_index("blk"), lax.axis_index("ga")
    y_hi, core = blk // 2, blk % 2
    x, y_lo, z = ga // 8, (ga // 4) % 2, ga % 4
    at_inner = x // 2 == y_hi
    near_plane = jnp.where(at_inner, x, 3 - x)
    near = core == near_plane % 2

    low, first = z < 2, y_lo == 0
    other = 1 - y_lo
    z_up, z_down, z_across = (z + 1) % 4, (z + 3) % 4, (z + 2) % 4
    table = [y_lo * 4 + z, y_lo * 4 + z_up, other * 4 + z_up]
    table += [jnp.where(low, y_lo, other) * 4 + z_across]
    table += [y_lo * 4 + z, y_lo * 4 + z_down, other * 4 + z_down]
    table += [jnp.where(low, other, y_lo) * 4 + z_across, other * 4 + z]
    table += [near, at_inner, at_inner & first]
    table = jnp.stack([entry.astype(jnp.int32) for entry in table])
    odd = x % 2
    sides = [first, ~first]
    factors_own = [jnp.where(at_inner, 0.5, 1.0), jnp.where(at_inner, 0.5, 0.0)] + sides
    factors_partner = [jnp.where(at_inner, odd, 1), jnp.where(at_inner, 1 - odd, 0)] + sides
    factors_own = jnp.stack([entry * jnp.float32(1) for entry in factors_own])
    factors_partner = jnp.stack([entry * jnp.float32(1) for entry in factors_partner])
    factors_here = jnp.where(near, factors_own, factors_partner)
    factors_there = jnp.where(near, factors_partner, factors_own)
    one = jnp.ones((1, bands * NS), pair_elements.dtype)
    weight = jnp.where(summed_bands < occupied[0], -0.5, 0.5).astype(pair_elements.dtype)
    weight = jnp.broadcast_to(jnp.repeat(weight, NS)[None, :], (16, bands * NS))

    held = lax.optimization_barrier
    own = pair_elements
    cut = rows * 11 // 16
    brought = send(jnp.concatenate([own, weight], 0), INJECT)
    own_side = send(own, SIDE_INNER)
    own_rows = own * weight[:1]
    partner_rows = send(own_rows, PARTNER)
    (
        brought, own_side, own_rows, partner_rows, far_1, far_2, table, factors_here, factors_there, one,
    ) = held(
        (
            brought, own_side, own_rows, partner_rows, screening[:cut], screening[cut:],
            table, factors_here, factors_there, one,
        )
    )

    swapped_1 = send(far_1, SWAP)
    brought_side = send(brought, SIDE)
    up_1 = send(blend(at_inner, own, brought[:rows]), DOWN)
    down_1 = send(brought, UP)
    native_side = blend(at_inner, own_side, brought_side[:rows])
    own_side, brought, brought_side, native_side, up_1, down_1, partner_rows = held(
        (own_side, brought, brought_side, native_side, up_1, down_1, partner_rows)
    )

    up_2 = send(native_side, DOWN)
    down_2 = send(brought_side, UP)
    foreign_rows = send(partner_rows, RETURN)
    brought_weight = jnp.where(at_inner, brought[rows : rows + 1], one)
    weight_here = jnp.where(near, brought_weight, one)
    weight_there = jnp.where(near, one, brought_weight)
    foreign_own = blend(at_inner, brought[:rows], own_rows)
    (
        swapped_1, foreign_rows, up_1, down_1, up_2, down_2, far_2,
        weight_here, weight_there, foreign_own,
    ) = held(
        (
            swapped_1, foreign_rows, up_1, down_1, up_2, down_2, far_2,
            weight_here, weight_there, foreign_own,
        )
    )

    swapped_2 = send(far_2, SWAP)
    across_up = send(blend((z + 3) % 4 < 2, up_1, up_2), DOWN)
    across_down = send(blend((z + 1) % 4 < 2, down_2, down_1), UP)
    foreign_partner = blend(at_inner, foreign_rows, partner_rows)
    swapped_1, swapped_2, across_up, across_down, near_w, foreign_partner = held(
        (swapped_1, swapped_2, across_up, across_down, screening, foreign_partner)
    )

    near_other = send(near_w, CORE_NEAR)
    swapped_other = [send(swapped_1, CORE_FAR), send(swapped_2, CORE_FAR)]
    blocks = [own, brought, own_side, brought_side, up_1, down_1, up_2, down_2]
    blocks += [across_up, across_down]
    half = products(
        table,
        factors_here,
        ([near_w], own_rows, foreign_own),
        ([swapped_1, swapped_2], partner_rows, foreign_partner),
        weight_here,
        blocks,
    )
    value = products(
        table,
        factors_there,
        (swapped_other, partner_rows, foreign_partner),
        ([near_other], own_rows, foreign_own),
        weight_there,
        blocks,
        half,
        scale,
    )
    parts = lax.all_to_all(value.reshape(NS, 1, NS), AXES, 0, 0)
    return jnp.sum(parts, 0)


def solution(mesh):
    placed = (P("ga", "blk"), P("ga", "blk"), P("blk"), P())
    return jax.shard_map(
        shards, mesh=mesh, in_specs=placed, out_specs=P(("blk", "ga"), None), check_vma=False
    )
```

```python
import math

import jax
import jax.numpy as jnp
from jax import lax
from jax.experimental import pallas as pl
from jax.experimental.pallas import tpu as pltpu
from jax.sharding import PartitionSpec as P

NS = 128
AXES = ("blk", "ga")


def place(x, y, z, core):
    return ((y // 2) * 2 + core) * 32 + (x % 4) * 8 + (y % 2) * 4 + z % 4


def pairs(target, keep=lambda x, y, z, core: True):
    return [
        (place(x, y, z, core), place(*target(x, y, z, core)))
        for x in range(4)
        for y in range(4)
        for z in range(4)
        for core in range(2)
        if keep(x, y, z, core)
    ]


def inner(x, y):
    return x // 2 == y // 2


def far_core(x, y):
    return 1 - (x if inner(x, y) else 3 - x) % 2


def is_inner(x, y, z, core):
    return inner(x, y)


def is_far(x, y, z, core):
    return core == far_core(x, y)


def to_near_plane(x, y, z, core):
    return (3 - x, y, z, core) if inner(x, y) else (x, (y + 2) % 4, z, core)


def to_partner(x, y, z, core):
    return x ^ 1, y, z, far_core(x ^ 1, y)


CORE_NEAR = pairs(
    lambda x, y, z, core: (x, y, z, 1 - core), lambda x, y, z, core: not is_far(x, y, z, core)
)
CORE_FAR = pairs(lambda x, y, z, core: (x, y, z, 1 - core), is_far)
INJECT = pairs(to_near_plane)
RETURN = pairs(to_near_plane, lambda x, y, z, core: not inner(x, y))
SWAP = pairs(to_partner, is_far)
PARTNER = pairs(lambda x, y, z, core: (x ^ 1, y, z, core))
SIDE = pairs(lambda x, y, z, core: (x, y ^ 1, z, core))
SIDE_INNER = pairs(lambda x, y, z, core: (x, y ^ 1, z, core), is_inner)


def down(x, y, z, core):
    return x, y, z - 1, core


def up(x, y, z, core):
    return x, y, z + 1, core


DOWN, UP = pairs(down), pairs(up)

SLOTS = 9
NEAR, INNER, SIDE_OWN, ROLE = range(SLOTS, SLOTS + 4)


def send(value, table):
    return lax.ppermute(value, AXES, table)


def blend(flag, yes, no):
    flag = flag.astype(yes.dtype)
    return yes * flag + no * (1 - flag)


def products(table, factors, near, far, weight_b, blocks, before=None, scale=None):
    (near_w, *near_rows), (far_w, *far_rows) = near, far
    parts = [len(near_w), len(far_w)]
    rows, (depth, width) = sum(part.shape[0] for part in near_w), blocks[0].shape
    bands = width // NS

    def kernel(table, factors, *refs):
        near_refs, refs = refs[: parts[0]], refs[parts[0] :]
        far_refs, refs = refs[: parts[1]], refs[parts[1] :]
        near_a, *near_b = refs[:3]
        far_a, *far_b = refs[3:6]
        weight_ref, refs = refs[6], refs[7:]
        own, brought, own_side, brought_side, up_1, down_1, up_2, down_2 = refs[:8]
        across_up, across_down = refs[8:10]
        refs = refs[10:]
        if before is not None:
            before_ref, refs = refs[0], refs[1:]
        out, w, q, left, sems = refs

        def choose(flag, yes, no):
            if yes is no:
                copy(*yes)
                return

            @pl.when(table[flag] == 1)
            def _():
                copy(*yes)

            @pl.when(table[flag] == 0)
            def _():
                copy(*no)

        def copy(*triples):
            for source, target, sem in triples:
                pltpu.make_async_copy(source, target, sem).start()

        def part(slot):
            return slot // 4, pl.ds((slot % 4) * depth, depth)

        sources = [
            (INNER, own, brought),
            (INNER, up_1, up_1),
            (INNER, up_2, up_2),
            (INNER, across_up, across_up),
            (INNER, brought, brought),
            (INNER, down_1, down_1),
            (INNER, down_2, down_2),
            (INNER, across_down, across_down),
            (SIDE_OWN, own_side, brought_side),
        ]
        for slot in (8, 0, 1, 2, 3, 4, 5, 6, 7):
            flag, yes, no = sources[slot]
            yes, no = yes.at[pl.ds(0, depth)], no.at[pl.ds(0, depth)] if no is not yes else None
            group, place_in = part(slot)
            target, sem = q.at[group, place_in], sems.at[0, group]
            if no is None:
                copy((yes, target, sem))
            else:
                choose(flag, [(yes, target, sem)], [(no, target, sem)])
            columns = pl.ds(pl.multiple_of(table[slot] * depth, depth), depth)
            copies = []
            for side in (near_refs, far_refs):
                at, triples = 0, []
                for ref in side:
                    target = w.at[group, pl.ds(at, ref.shape[0]), place_in]
                    triples.append((ref.at[:, columns], target, sems.at[1, group]))
                    at += ref.shape[0]
                copies.append(triples)
            choose(NEAR, *copies)
        block = pl.ds(0, rows)
        target, sem = left.at[0], sems.at[0, 3]
        choose(NEAR, [(near_a.at[block], target, sem)], [(far_a.at[block], target, sem)])
        target, sem = left.at[1], sems.at[1, 3]
        for role, source in enumerate((far_b[1], far_b[0], near_b[1], near_b[0])):

            @pl.when(table[ROLE] == role)
            def _(source=source):
                copy((source.at[block], target, sem))

        def wait(ref, sem):
            pltpu.make_async_copy(ref, ref, sem).wait()

        wait(q.at[2, pl.ds(0, depth)], sems.at[0, 2])
        wait(w.at[2, :, pl.ds(0, depth)], sems.at[1, 2])
        side = jnp.dot(w[2, :, :depth], q[2, :depth], preferred_element_type=jnp.float32)
        result = jnp.zeros((NS, 2 * NS), jnp.float32)
        for group in range(2):
            wait(q.at[group], sems.at[0, group])
            wait(w.at[group], sems.at[1, group])
            q[group, :depth] = q[group, :depth] * factors[group].astype(q.dtype)
            total = jnp.dot(w[group], q[group], preferred_element_type=jnp.float32)
            total = total + side * factors[2 + group]
            if group == 1:
                total = total * weight_ref[0:1, :].astype(jnp.float32)
            high = total.astype(jnp.bfloat16)
            low = (total - high.astype(jnp.float32)).astype(jnp.bfloat16)
            wait(left.at[group], sems.at[group, 3])
            for band in range(bands):
                lanes = slice(band * NS, (band + 1) * NS)
                result = result + lax.dot_general(
                    left[group, :, lanes],
                    jnp.concatenate([high[:, lanes], low[:, lanes]], 1),
                    (((0,), (0,)), ((), ())),
                    preferred_element_type=jnp.float32,
                )
        result = result[:, :NS] + result[:, NS:]
        if before is not None:
            result = result + before_ref[...]
            result = (result + result.T) * jnp.float32(scale)
        out[...] = result

    hbm = pl.BlockSpec(memory_space=pl.ANY)
    vmem = pl.BlockSpec(memory_space=pltpu.VMEM)
    smem = pl.BlockSpec(memory_space=pltpu.SMEM)
    more = [] if before is None else [before]
    return pl.pallas_call(
        kernel,
        out_shape=jax.ShapeDtypeStruct((NS, NS), jnp.float32),
        in_specs=[smem, smem] + [hbm] * (sum(parts) + 6) + [vmem] + [hbm] * 10 + [vmem] * len(more),
        out_specs=vmem,
        scratch_shapes=[
            pltpu.VMEM((3, rows, 4 * depth), jnp.bfloat16),
            pltpu.VMEM((3, 4 * depth, width), jnp.bfloat16),
            pltpu.VMEM((2, rows, width), jnp.bfloat16),
            pltpu.SemaphoreType.DMA((2, 4)),
        ],
        compiler_params=pltpu.CompilerParams(vmem_limit_bytes=60 * 1024 * 1024),
        cost_estimate=pl.CostEstimate(
            flops=2 * SLOTS * rows * depth * width,
            bytes_accessed=2 * SLOTS * (rows + width) * depth,
            transcendentals=0,
        ),
    )(table, factors, *near_w, *far_w, *near_rows, *far_rows, weight_b, *blocks, *more)


def shards(screening, pair_elements, summed_bands, occupied):
    rows = pair_elements.shape[0]
    bands = summed_bands.shape[0]
    total_g = rows * lax.axis_size("ga")
    scale = 1.0 / math.sqrt(total_g * bands * lax.axis_size("blk"))
    blk, ga = lax.axis_index("blk"), lax.axis_index("ga")
    y_hi, core = blk // 2, blk % 2
    x, y_lo, z = ga // 8, (ga // 4) % 2, ga % 4
    at_inner = x // 2 == y_hi
    near_plane = jnp.where(at_inner, x, 3 - x)
    near = core == near_plane % 2

    low, first = z < 2, y_lo == 0
    other = 1 - y_lo
    z_up, z_down, z_across = (z + 1) % 4, (z + 3) % 4, (z + 2) % 4
    table = [y_lo * 4 + z, y_lo * 4 + z_up, other * 4 + z_up]
    table += [jnp.where(low, y_lo, other) * 4 + z_across]
    table += [y_lo * 4 + z, y_lo * 4 + z_down, other * 4 + z_down]
    table += [jnp.where(low, other, y_lo) * 4 + z_across, other * 4 + z]
    table += [near, at_inner, at_inner & first, near * 2 + at_inner]
    table = jnp.stack([entry.astype(jnp.int32) for entry in table])
    odd = x % 2
    sides = [first, ~first]
    factors_own = [jnp.where(at_inner, 0.5, 1.0), jnp.where(at_inner, 0.5, 0.0)] + sides
    factors_partner = [jnp.where(at_inner, odd, 1), jnp.where(at_inner, 1 - odd, 0)] + sides
    factors_own = jnp.stack([entry * jnp.float32(1) for entry in factors_own])
    factors_partner = jnp.stack([entry * jnp.float32(1) for entry in factors_partner])
    factors_here = jnp.where(near, factors_own, factors_partner)
    factors_there = jnp.where(near, factors_partner, factors_own)
    one = jnp.ones((1, bands * NS), pair_elements.dtype)
    weight = jnp.where(summed_bands < occupied[0], -0.5, 0.5).astype(pair_elements.dtype)
    weight = jnp.broadcast_to(jnp.repeat(weight, NS)[None, :], (16, bands * NS))

    held = lax.optimization_barrier
    own = pair_elements
    cut = rows * 11 // 16
    brought = send(jnp.concatenate([own, weight], 0), INJECT)
    own_side = send(own, SIDE_INNER)
    own_rows = own * weight[:1]
    partner_rows = send(own_rows, PARTNER)
    (
        near_w, brought, own_side, partner_rows, own_rows, far_1, far_2,
        table, factors_here, factors_there, one,
    ) = held(
        (
            screening, brought, own_side, partner_rows, own_rows, screening[:cut], screening[cut:],
            table, factors_here, factors_there, one,
        )
    )

    swapped_1 = send(far_1, SWAP)
    brought_side = send(brought, SIDE)
    up_1 = send(blend(at_inner, own, brought[:rows]), DOWN)
    down_1 = send(brought, UP)
    native_side = blend(at_inner, own_side, brought_side[:rows])
    own_side, brought, brought_side, native_side, up_1, down_1, partner_rows, near_w = held(
        (own_side, brought, brought_side, native_side, up_1, down_1, partner_rows, near_w)
    )

    up_2 = send(native_side, DOWN)
    down_2 = send(brought_side, UP)
    brought_weight = jnp.where(at_inner, brought[rows : rows + 1], one)
    weight_here = jnp.where(near, brought_weight, one)
    weight_there = jnp.where(near, one, brought_weight)
    foreign_rows = send(partner_rows, RETURN)
    swapped_1, foreign_rows, up_1, down_1, up_2, down_2, far_2, weight_here, weight_there, near_w = held(
        (swapped_1, foreign_rows, up_1, down_1, up_2, down_2, far_2, weight_here, weight_there, near_w)
    )

    swapped_2 = send(far_2, SWAP)
    across_up = send(blend((z + 3) % 4 < 2, up_1, up_2), DOWN)
    across_down = send(blend((z + 1) % 4 < 2, down_2, down_1), UP)
    near_other = send(near_w, CORE_NEAR)
    swapped_1, swapped_2, across_up, across_down, foreign_rows, near_other = held(
        (swapped_1, swapped_2, across_up, across_down, foreign_rows, near_other)
    )

    swapped_other = [send(swapped_1, CORE_FAR), send(swapped_2, CORE_FAR)]
    blocks = [own, brought, own_side, brought_side, up_1, down_1, up_2, down_2]
    blocks += [across_up, across_down]
    half = products(
        table,
        factors_here,
        ([screening], own_rows, brought, own_rows),
        ([swapped_1, swapped_2], partner_rows, foreign_rows, partner_rows),
        weight_here,
        blocks,
    )
    value = products(
        table,
        factors_there,
        (swapped_other, partner_rows, foreign_rows, partner_rows),
        ([near_other], own_rows, brought, own_rows),
        weight_there,
        blocks,
        half,
        scale,
    )
    parts = lax.all_to_all(value.reshape(NS, 1, NS), AXES, 0, 0)
    return jnp.sum(parts, 0)


def solution(mesh):
    placed = (P("ga", "blk"), P("ga", "blk"), P("blk"), P())
    return jax.shard_map(
        shards, mesh=mesh, in_specs=placed, out_specs=P(("blk", "ga"), None), check_vma=False
    )
```

```python
import math

import jax
import jax.numpy as jnp
from jax import lax
from jax.experimental import pallas as pl
from jax.experimental.pallas import tpu as pltpu
from jax.sharding import PartitionSpec as P

NS = 128
AXES = ("blk", "ga")


def place(x, y, z, core):
    return ((y // 2) * 2 + core) * 32 + (x % 4) * 8 + (y % 2) * 4 + z % 4


def pairs(target, keep=lambda x, y, z, core: True):
    return [
        (place(x, y, z, core), place(*target(x, y, z, core)))
        for x in range(4)
        for y in range(4)
        for z in range(4)
        for core in range(2)
        if keep(x, y, z, core)
    ]


def inner(x, y):
    return x // 2 == y // 2


def far_core(x, y):
    return 1 - (x if inner(x, y) else 3 - x) % 2


def is_inner(x, y, z, core):
    return inner(x, y)


def is_far(x, y, z, core):
    return core == far_core(x, y)


def to_near_plane(x, y, z, core):
    return (3 - x, y, z, core) if inner(x, y) else (x, (y + 2) % 4, z, core)


def to_partner(x, y, z, core):
    return x ^ 1, y, z, far_core(x ^ 1, y)


CORE_NEAR = pairs(
    lambda x, y, z, core: (x, y, z, 1 - core), lambda x, y, z, core: not is_far(x, y, z, core)
)
CORE_FAR = pairs(lambda x, y, z, core: (x, y, z, 1 - core), is_far)
INJECT = pairs(to_near_plane)
RETURN = pairs(to_near_plane, lambda x, y, z, core: not inner(x, y))
SWAP = pairs(to_partner, is_far)
PARTNER = pairs(lambda x, y, z, core: (x ^ 1, y, z, core))
SIDE = pairs(lambda x, y, z, core: (x, y ^ 1, z, core))
SIDE_INNER = pairs(lambda x, y, z, core: (x, y ^ 1, z, core), is_inner)


def down(x, y, z, core):
    return x, y, z - 1, core


def up(x, y, z, core):
    return x, y, z + 1, core


DOWN, UP = pairs(down), pairs(up)

SLOTS = 9
NEAR, INNER, SIDE_OWN, ROLE = range(SLOTS, SLOTS + 4)


def send(value, table):
    return lax.ppermute(value, AXES, table)


def blend(flag, yes, no):
    flag = flag.astype(yes.dtype)
    return yes * flag + no * (1 - flag)


def products(table, factors, near, far, weight_b, blocks, before=None, scale=None):
    (near_w, *near_rows), (far_w, *far_rows) = near, far
    parts = [len(near_w), len(far_w)]
    rows, (depth, width) = sum(part.shape[0] for part in near_w), blocks[0].shape
    bands = width // NS

    def kernel(table, factors, *refs):
        near_refs, refs = refs[: parts[0]], refs[parts[0] :]
        far_refs, refs = refs[: parts[1]], refs[parts[1] :]
        near_a, *near_b = refs[:3]
        far_a, *far_b = refs[3:6]
        weight_ref, refs = refs[6], refs[7:]
        own, brought, own_side, brought_side, up_1, down_1, up_2, down_2 = refs[:8]
        across_up, across_down = refs[8:10]
        refs = refs[10:]
        if before is not None:
            before_ref, refs = refs[0], refs[1:]
        out, w, q, left, sems = refs

        def choose(flag, yes, no):
            if yes is no:
                copy(*yes)
                return

            @pl.when(table[flag] == 1)
            def _():
                copy(*yes)

            @pl.when(table[flag] == 0)
            def _():
                copy(*no)

        def copy(*triples):
            for source, target, sem in triples:
                pltpu.make_async_copy(source, target, sem).start()

        def part(slot):
            return slot // 4, pl.ds((slot % 4) * depth, depth)

        sources = [
            (INNER, own, brought),
            (INNER, up_1, up_1),
            (INNER, up_2, up_2),
            (INNER, across_up, across_up),
            (INNER, brought, brought),
            (INNER, down_1, down_1),
            (INNER, down_2, down_2),
            (INNER, across_down, across_down),
            (SIDE_OWN, own_side, brought_side),
        ]
        for slot in (8, 0, 1, 2, 3, 4, 5, 6, 7):
            flag, yes, no = sources[slot]
            yes, no = yes.at[pl.ds(0, depth)], no.at[pl.ds(0, depth)] if no is not yes else None
            group, place_in = part(slot)
            target, sem = q.at[group, place_in], sems.at[0, group]
            if no is None:
                copy((yes, target, sem))
            else:
                choose(flag, [(yes, target, sem)], [(no, target, sem)])
            columns = pl.ds(pl.multiple_of(table[slot] * depth, depth), depth)
            copies = []
            for side in (near_refs, far_refs):
                at, triples = 0, []
                for ref in side:
                    target = w.at[group, pl.ds(at, ref.shape[0]), place_in]
                    triples.append((ref.at[:, columns], target, sems.at[1, group]))
                    at += ref.shape[0]
                copies.append(triples)
            choose(NEAR, *copies)
        block = pl.ds(0, rows)
        target, sem = left.at[0], sems.at[0, 3]
        choose(NEAR, [(near_a.at[block], target, sem)], [(far_a.at[block], target, sem)])
        target, sem = left.at[1], sems.at[1, 3]
        for role, source in enumerate((far_b[1], far_b[0], near_b[1], near_b[0])):

            @pl.when(table[ROLE] == role)
            def _(source=source):
                copy((source.at[block], target, sem))

        def wait(ref, sem):
            pltpu.make_async_copy(ref, ref, sem).wait()

        wait(q.at[2, pl.ds(0, depth)], sems.at[0, 2])
        wait(w.at[2, :, pl.ds(0, depth)], sems.at[1, 2])
        side = jnp.dot(w[2, :, :depth], q[2, :depth], preferred_element_type=jnp.float32)
        result = jnp.zeros((NS, 2 * NS), jnp.float32)
        for group in range(2):
            wait(q.at[group], sems.at[0, group])
            wait(w.at[group], sems.at[1, group])
            q[group, :depth] = q[group, :depth] * factors[group].astype(q.dtype)
            total = jnp.dot(w[group], q[group], preferred_element_type=jnp.float32)
            total = total + side * factors[2 + group]
            if group == 1:
                total = total * weight_ref[0:1, :].astype(jnp.float32)
            high = total.astype(jnp.bfloat16)
            low = (total - high.astype(jnp.float32)).astype(jnp.bfloat16)
            wait(left.at[group], sems.at[group, 3])
            for band in range(bands):
                lanes = slice(band * NS, (band + 1) * NS)
                result = result + lax.dot_general(
                    left[group, :, lanes],
                    jnp.concatenate([high[:, lanes], low[:, lanes]], 1),
                    (((0,), (0,)), ((), ())),
                    preferred_element_type=jnp.float32,
                )
        result = result[:, :NS] + result[:, NS:]
        if before is not None:
            result = result + before_ref[...]
            result = (result + result.T) * jnp.float32(scale)
        out[...] = result

    hbm = pl.BlockSpec(memory_space=pl.ANY)
    vmem = pl.BlockSpec(memory_space=pltpu.VMEM)
    smem = pl.BlockSpec(memory_space=pltpu.SMEM)
    more = [] if before is None else [before]
    return pl.pallas_call(
        kernel,
        out_shape=jax.ShapeDtypeStruct((NS, NS), jnp.float32),
        in_specs=[smem, smem] + [hbm] * (sum(parts) + 6) + [vmem] + [hbm] * 10 + [vmem] * len(more),
        out_specs=vmem,
        scratch_shapes=[
            pltpu.VMEM((3, rows, 4 * depth), jnp.bfloat16),
            pltpu.VMEM((3, 4 * depth, width), jnp.bfloat16),
            pltpu.VMEM((2, rows, width), jnp.bfloat16),
            pltpu.SemaphoreType.DMA((2, 4)),
        ],
        compiler_params=pltpu.CompilerParams(vmem_limit_bytes=63 * 1024 * 1024),
        cost_estimate=pl.CostEstimate(
            flops=2 * SLOTS * rows * depth * width,
            bytes_accessed=2 * SLOTS * (rows + width) * depth,
            transcendentals=0,
        ),
    )(table, factors, *near_w, *far_w, *near_rows, *far_rows, weight_b, *blocks, *more)


def shards(screening, pair_elements, summed_bands, occupied):
    rows = pair_elements.shape[0]
    bands = summed_bands.shape[0]
    total_g = rows * lax.axis_size("ga")
    scale = 1.0 / math.sqrt(total_g * bands * lax.axis_size("blk"))
    blk, ga = lax.axis_index("blk"), lax.axis_index("ga")
    y_hi, core = blk // 2, blk % 2
    x, y_lo, z = ga // 8, (ga // 4) % 2, ga % 4
    at_inner = x // 2 == y_hi
    near_plane = jnp.where(at_inner, x, 3 - x)
    near = core == near_plane % 2

    low, first = z < 2, y_lo == 0
    other = 1 - y_lo
    z_up, z_down, z_across = (z + 1) % 4, (z + 3) % 4, (z + 2) % 4
    table = [y_lo * 4 + z, y_lo * 4 + z_up, other * 4 + z_up]
    table += [jnp.where(low, y_lo, other) * 4 + z_across]
    table += [y_lo * 4 + z, y_lo * 4 + z_down, other * 4 + z_down]
    table += [jnp.where(low, other, y_lo) * 4 + z_across, other * 4 + z]
    table += [near, at_inner, at_inner & first, near * 2 + at_inner]
    table = jnp.stack([entry.astype(jnp.int32) for entry in table])
    odd = x % 2
    sides = [first, ~first]
    factors_own = [jnp.where(at_inner, 0.5, 1.0), jnp.where(at_inner, 0.5, 0.0)] + sides
    factors_partner = [jnp.where(at_inner, odd, 1), jnp.where(at_inner, 1 - odd, 0)] + sides
    factors_own = jnp.stack([entry * jnp.float32(1) for entry in factors_own])
    factors_partner = jnp.stack([entry * jnp.float32(1) for entry in factors_partner])
    factors_here = jnp.where(near, factors_own, factors_partner)
    factors_there = jnp.where(near, factors_partner, factors_own)
    one = jnp.ones((1, bands * NS), pair_elements.dtype)
    weight = jnp.where(summed_bands < occupied[0], -0.5, 0.5).astype(pair_elements.dtype)
    weight = jnp.broadcast_to(jnp.repeat(weight, NS)[None, :], (16, bands * NS))

    held = lax.optimization_barrier
    own = pair_elements
    cut = rows * 11 // 16
    brought = send(jnp.concatenate([own, weight], 0), INJECT)
    own_side = send(own, SIDE_INNER)
    own_rows = own * weight[:1]
    partner_rows = send(own_rows, PARTNER)
    (
        near_w, brought, own_side, partner_rows, own_rows, far_1, far_2,
        table, factors_here, factors_there, one,
    ) = held(
        (
            screening, brought, own_side, partner_rows, own_rows, screening[:cut], screening[cut:],
            table, factors_here, factors_there, one,
        )
    )

    swapped_1 = send(far_1, SWAP)
    brought_side = send(brought, SIDE)
    up_1 = send(blend(at_inner, own, brought[:rows]), DOWN)
    down_1 = send(brought, UP)
    native_side = blend(at_inner, own_side, brought_side[:rows])
    own_side, brought, brought_side, native_side, up_1, down_1, partner_rows, near_w = held(
        (own_side, brought, brought_side, native_side, up_1, down_1, partner_rows, near_w)
    )

    up_2 = send(native_side, DOWN)
    down_2 = send(brought_side, UP)
    brought_weight = jnp.where(at_inner, brought[rows : rows + 1], one)
    weight_here = jnp.where(near, brought_weight, one)
    weight_there = jnp.where(near, one, brought_weight)
    foreign_rows = send(partner_rows, RETURN)
    swapped_1, foreign_rows, up_1, down_1, up_2, down_2, far_2, weight_here, weight_there, near_w = held(
        (swapped_1, foreign_rows, up_1, down_1, up_2, down_2, far_2, weight_here, weight_there, near_w)
    )

    swapped_2 = send(far_2, SWAP)
    across_up = send(blend((z + 3) % 4 < 2, up_1, up_2), DOWN)
    across_down = send(blend((z + 1) % 4 < 2, down_2, down_1), UP)
    near_other = send(near_w, CORE_NEAR)
    swapped_1, swapped_2, across_up, across_down, foreign_rows, near_other = held(
        (swapped_1, swapped_2, across_up, across_down, foreign_rows, near_other)
    )

    swapped_other = [send(swapped_1, CORE_FAR), send(swapped_2, CORE_FAR)]
    blocks = [own, brought, own_side, brought_side, up_1, down_1, up_2, down_2]
    blocks += [across_up, across_down]
    half = products(
        table,
        factors_here,
        ([screening], own_rows, brought, own_rows),
        ([swapped_1, swapped_2], partner_rows, foreign_rows, partner_rows),
        weight_here,
        blocks,
    )
    value = products(
        table,
        factors_there,
        (swapped_other, partner_rows, foreign_rows, partner_rows),
        ([near_other], own_rows, brought, own_rows),
        weight_there,
        blocks,
        half,
        scale,
    )
    parts = lax.all_to_all(value.reshape(NS, 1, NS), AXES, 0, 0)
    return jnp.sum(parts, 0)


def solution(mesh):
    placed = (P("ga", "blk"), P("ga", "blk"), P("blk"), P())
    return jax.shard_map(
        shards, mesh=mesh, in_specs=placed, out_specs=P(("blk", "ga"), None), check_vma=False
    )
```

```python
import math

import jax
import jax.numpy as jnp
from jax import lax
from jax.experimental import pallas as pl
from jax.experimental.pallas import tpu as pltpu
from jax.sharding import PartitionSpec as P

NS = 128
AXES = ("blk", "ga")


def place(x, y, z, core):
    return ((y // 2) * 2 + core) * 32 + (x % 4) * 8 + (y % 2) * 4 + z % 4


def pairs(target, keep=lambda x, y, z, core: True):
    return [
        (place(x, y, z, core), place(*target(x, y, z, core)))
        for x in range(4)
        for y in range(4)
        for z in range(4)
        for core in range(2)
        if keep(x, y, z, core)
    ]


def inner(x, y):
    return x // 2 == y // 2


def far_core(x, y):
    return 1 - (x if inner(x, y) else 3 - x) % 2


def is_inner(x, y, z, core):
    return inner(x, y)


def is_far(x, y, z, core):
    return core == far_core(x, y)


def to_near_plane(x, y, z, core):
    return (3 - x, y, z, core) if inner(x, y) else (x, (y + 2) % 4, z, core)


def to_partner(x, y, z, core):
    return x ^ 1, y, z, far_core(x ^ 1, y)


CORE_NEAR = pairs(
    lambda x, y, z, core: (x, y, z, 1 - core), lambda x, y, z, core: not is_far(x, y, z, core)
)
CORE_FAR = pairs(lambda x, y, z, core: (x, y, z, 1 - core), is_far)
INJECT = pairs(to_near_plane)
RETURN = pairs(to_near_plane, lambda x, y, z, core: not inner(x, y))
SWAP = pairs(to_partner, is_far)
PARTNER = pairs(lambda x, y, z, core: (x ^ 1, y, z, core))
SIDE = pairs(lambda x, y, z, core: (x, y ^ 1, z, core))
SIDE_INNER = pairs(lambda x, y, z, core: (x, y ^ 1, z, core), is_inner)


def down(x, y, z, core):
    return x, y, z - 1, core


def up(x, y, z, core):
    return x, y, z + 1, core


DOWN, UP = pairs(down), pairs(up)

SLOTS = 9
NEAR, INNER, SIDE_OWN, ROLE = range(SLOTS, SLOTS + 4)


def send(value, table):
    return lax.ppermute(value, AXES, table)


def blend(flag, yes, no):
    flag = flag.astype(yes.dtype)
    return yes * flag + no * (1 - flag)


def products(table, factors, near, far, weight_b, blocks, before=None, scale=None):
    (near_w, *near_rows), (far_w, *far_rows) = near, far
    parts = [len(near_w), len(far_w)]
    rows, (depth, width) = sum(part.shape[0] for part in near_w), blocks[0].shape
    bands = width // NS

    def kernel(table, factors, *refs):
        near_refs, refs = refs[: parts[0]], refs[parts[0] :]
        far_refs, refs = refs[: parts[1]], refs[parts[1] :]
        near_a, *near_b = refs[:3]
        far_a, *far_b = refs[3:6]
        weight_ref, refs = refs[6], refs[7:]
        own, brought, own_side, brought_side, up_1, down_1, up_2, down_2 = refs[:8]
        across_up, across_down = refs[8:10]
        refs = refs[10:]
        if before is not None:
            before_ref, refs = refs[0], refs[1:]
        out, w, q, left, sems = refs

        def choose(flag, yes, no):
            if yes is no:
                copy(*yes)
                return

            @pl.when(table[flag] == 1)
            def _():
                copy(*yes)

            @pl.when(table[flag] == 0)
            def _():
                copy(*no)

        def copy(*triples):
            for source, target, sem in triples:
                pltpu.make_async_copy(source, target, sem).start()

        def part(slot):
            return slot // 4, pl.ds((slot % 4) * depth, depth)

        sources = [
            (INNER, own, brought),
            (INNER, up_1, up_1),
            (INNER, up_2, up_2),
            (INNER, across_up, across_up),
            (INNER, brought, brought),
            (INNER, down_1, down_1),
            (INNER, down_2, down_2),
            (INNER, across_down, across_down),
            (SIDE_OWN, own_side, brought_side),
        ]
        for slot in (8, 0, 1, 2, 3, 4, 5, 6, 7):
            flag, yes, no = sources[slot]
            yes, no = yes.at[pl.ds(0, depth)], no.at[pl.ds(0, depth)] if no is not yes else None
            group, place_in = part(slot)
            target, sem = q.at[group, place_in], sems.at[0, group]
            if no is None:
                copy((yes, target, sem))
            else:
                choose(flag, [(yes, target, sem)], [(no, target, sem)])
            columns = pl.ds(pl.multiple_of(table[slot] * depth, depth), depth)
            if slot == 4:
                continue
            copies = []
            for side in (near_refs, far_refs):
                at, triples = 0, []
                for ref in side:
                    target = w.at[group, pl.ds(at, ref.shape[0]), place_in]
                    triples.append((ref.at[:, columns], target, sems.at[1, group]))
                    at += ref.shape[0]
                copies.append(triples)
            choose(NEAR, *copies)
        block = pl.ds(0, rows)
        target, sem = left.at[0], sems.at[0, 3]
        choose(NEAR, [(near_a.at[block], target, sem)], [(far_a.at[block], target, sem)])
        target, sem = left.at[1], sems.at[1, 3]
        for role, source in enumerate((far_b[1], far_b[0], near_b[1], near_b[0])):

            @pl.when(table[ROLE] == role)
            def _(source=source):
                copy((source.at[block], target, sem))

        def wait(ref, sem):
            pltpu.make_async_copy(ref, ref, sem).wait()

        wait(q.at[2, pl.ds(0, depth)], sems.at[0, 2])
        wait(w.at[2, :, pl.ds(0, depth)], sems.at[1, 2])
        side = jnp.dot(w[2, :, :depth], q[2, :depth], preferred_element_type=jnp.float32)
        result = jnp.zeros((NS, 2 * NS), jnp.float32)
        for group in range(2):
            wait(q.at[group], sems.at[0, group])
            rest = pl.ds(group * depth, (4 - group) * depth)
            wait(w.at[group, :, rest], sems.at[1, group])
            q[group, :depth] = q[group, :depth] * factors[group].astype(q.dtype)
            total = jnp.dot(w[group, :, rest], q[group, rest], preferred_element_type=jnp.float32)
            if group == 1:
                total = total + jnp.dot(
                    w[0, :, :depth], q[group, :depth], preferred_element_type=jnp.float32
                )
            total = total + side * factors[2 + group]
            if group == 1:
                total = total * weight_ref[0:1, :].astype(jnp.float32)
            high = total.astype(jnp.bfloat16)
            low = (total - high.astype(jnp.float32)).astype(jnp.bfloat16)
            wait(left.at[group], sems.at[group, 3])
            for band in range(bands):
                lanes = slice(band * NS, (band + 1) * NS)
                result = result + lax.dot_general(
                    left[group, :, lanes],
                    jnp.concatenate([high[:, lanes], low[:, lanes]], 1),
                    (((0,), (0,)), ((), ())),
                    preferred_element_type=jnp.float32,
                )
        result = result[:, :NS] + result[:, NS:]
        if before is not None:
            result = result + before_ref[...]
            result = (result + result.T) * jnp.float32(scale)
        out[...] = result

    hbm = pl.BlockSpec(memory_space=pl.ANY)
    vmem = pl.BlockSpec(memory_space=pltpu.VMEM)
    smem = pl.BlockSpec(memory_space=pltpu.SMEM)
    more = [] if before is None else [before]
    return pl.pallas_call(
        kernel,
        out_shape=jax.ShapeDtypeStruct((NS, NS), jnp.float32),
        in_specs=[smem, smem] + [hbm] * (sum(parts) + 6) + [vmem] + [hbm] * 10 + [vmem] * len(more),
        out_specs=vmem,
        scratch_shapes=[
            pltpu.VMEM((3, rows, 4 * depth), jnp.bfloat16),
            pltpu.VMEM((3, 4 * depth, width), jnp.bfloat16),
            pltpu.VMEM((2, rows, width), jnp.bfloat16),
            pltpu.SemaphoreType.DMA((2, 4)),
        ],
        compiler_params=pltpu.CompilerParams(vmem_limit_bytes=63 * 1024 * 1024),
        cost_estimate=pl.CostEstimate(
            flops=2 * SLOTS * rows * depth * width,
            bytes_accessed=2 * SLOTS * (rows + width) * depth,
            transcendentals=0,
        ),
    )(table, factors, *near_w, *far_w, *near_rows, *far_rows, weight_b, *blocks, *more)


def shards(screening, pair_elements, summed_bands, occupied):
    rows = pair_elements.shape[0]
    bands = summed_bands.shape[0]
    total_g = rows * lax.axis_size("ga")
    scale = 1.0 / math.sqrt(total_g * bands * lax.axis_size("blk"))
    blk, ga = lax.axis_index("blk"), lax.axis_index("ga")
    y_hi, core = blk // 2, blk % 2
    x, y_lo, z = ga // 8, (ga // 4) % 2, ga % 4
    at_inner = x // 2 == y_hi
    near_plane = jnp.where(at_inner, x, 3 - x)
    near = core == near_plane % 2

    low, first = z < 2, y_lo == 0
    other = 1 - y_lo
    z_up, z_down, z_across = (z + 1) % 4, (z + 3) % 4, (z + 2) % 4
    table = [y_lo * 4 + z, y_lo * 4 + z_up, other * 4 + z_up]
    table += [jnp.where(low, y_lo, other) * 4 + z_across]
    table += [y_lo * 4 + z, y_lo * 4 + z_down, other * 4 + z_down]
    table += [jnp.where(low, other, y_lo) * 4 + z_across, other * 4 + z]
    table += [near, at_inner, at_inner & first, near * 2 + at_inner]
    table = jnp.stack([entry.astype(jnp.int32) for entry in table])
    odd = x % 2
    sides = [first, ~first]
    factors_own = [jnp.where(at_inner, 0.5, 1.0), jnp.where(at_inner, 0.5, 0.0)] + sides
    factors_partner = [jnp.where(at_inner, odd, 1), jnp.where(at_inner, 1 - odd, 0)] + sides
    factors_own = jnp.stack([entry * jnp.float32(1) for entry in factors_own])
    factors_partner = jnp.stack([entry * jnp.float32(1) for entry in factors_partner])
    factors_here = jnp.where(near, factors_own, factors_partner)
    factors_there = jnp.where(near, factors_partner, factors_own)
    one = jnp.ones((1, bands * NS), pair_elements.dtype)
    weight = jnp.where(summed_bands < occupied[0], -0.5, 0.5).astype(pair_elements.dtype)
    weight = jnp.broadcast_to(jnp.repeat(weight, NS)[None, :], (16, bands * NS))

    held = lax.optimization_barrier
    own = pair_elements
    cut = rows * 11 // 16
    brought = send(jnp.concatenate([own, weight], 0), INJECT)
    own_side = send(own, SIDE_INNER)
    own_rows = own * weight[:1]
    partner_rows = send(own_rows, PARTNER)
    (
        near_w, brought, own_side, partner_rows, own_rows, far_1, far_2,
        table, factors_here, factors_there, one,
    ) = held(
        (
            screening, brought, own_side, partner_rows, own_rows, screening[:cut], screening[cut:],
            table, factors_here, factors_there, one,
        )
    )

    swapped_1 = send(far_1, SWAP)
    brought_side = send(brought, SIDE)
    up_1 = send(blend(at_inner, own, brought[:rows]), DOWN)
    down_1 = send(brought, UP)
    native_side = blend(at_inner, own_side, brought_side[:rows])
    own_side, brought, brought_side, native_side, up_1, down_1, partner_rows, near_w = held(
        (own_side, brought, brought_side, native_side, up_1, down_1, partner_rows, near_w)
    )

    up_2 = send(native_side, DOWN)
    down_2 = send(brought_side, UP)
    brought_weight = jnp.where(at_inner, brought[rows : rows + 1], one)
    weight_here = jnp.where(near, brought_weight, one)
    weight_there = jnp.where(near, one, brought_weight)
    foreign_rows = send(partner_rows, RETURN)
    swapped_1, foreign_rows, up_1, down_1, up_2, down_2, far_2, weight_here, weight_there, near_w = held(
        (swapped_1, foreign_rows, up_1, down_1, up_2, down_2, far_2, weight_here, weight_there, near_w)
    )

    swapped_2 = send(far_2, SWAP)
    across_up = send(blend((z + 3) % 4 < 2, up_1, up_2), DOWN)
    across_down = send(blend((z + 1) % 4 < 2, down_2, down_1), UP)
    near_other = send(near_w, CORE_NEAR)
    swapped_1, swapped_2, across_up, across_down, foreign_rows, near_other = held(
        (swapped_1, swapped_2, across_up, across_down, foreign_rows, near_other)
    )

    swapped_other = [send(swapped_1, CORE_FAR), send(swapped_2, CORE_FAR)]
    blocks = [own, brought, own_side, brought_side, up_1, down_1, up_2, down_2]
    blocks += [across_up, across_down]
    half = products(
        table,
        factors_here,
        ([screening], own_rows, brought, own_rows),
        ([swapped_1, swapped_2], partner_rows, foreign_rows, partner_rows),
        weight_here,
        blocks,
    )
    value = products(
        table,
        factors_there,
        (swapped_other, partner_rows, foreign_rows, partner_rows),
        ([near_other], own_rows, brought, own_rows),
        weight_there,
        blocks,
        half,
        scale,
    )
    parts = lax.all_to_all(value.reshape(NS, 1, NS), AXES, 0, 0)
    return jnp.sum(parts, 0)


def solution(mesh):
    placed = (P("ga", "blk"), P("ga", "blk"), P("blk"), P())
    return jax.shard_map(
        shards, mesh=mesh, in_specs=placed, out_specs=P(("blk", "ga"), None), check_vma=False
    )
```
